256 devices in a mesh: gx: 32 (over y, z_lo, core), gy: 8 (over x, z_hi).
Axes of the slice: x: 4, y: 4, z: 8 (z_hi: 2, z_lo: 4; z = z_hi * 4 + z_lo), core: 2. Of those that a mesh axis runs over, the one named last changes fastest.
Arguments:
- phase_fields: float32 [16, 512, 128, 128], P(None, 'gx', 'gy'), may hold values from 0 to 1, as said below
- grain_ids: int32 [32, 8, 8, 16], P('gx', 'gy'), may hold values from -1 to 4095, as said below
Outputs:
- phase_out: float32 [16, 512, 128, 128], P(None, 'gx', 'gy')
The draws below stay inside these ranges and needn't reach their ends.
Inputs may be any that keep to these rules, and one draw needn't show every extreme that they name: `grain_ids`: A tile lists distinct grains; between 5 * 16 / 8 (rounded down) and 15 slots are active, in random slots; every grain is listed by some tile, and grains of adjacent tiles appear in several tiles. `phase_fields`: the field of an empty slot is zero in the whole tile.
All inputs are finite; a program needn't handle non-finite values.
Results may differ from the reference program's by a relative error of at most 0.0001.
Values sent between devices are 32-bit elements; how exact they have to be, the bound alone decides.
No kernel may reach another device: no remote copies, remote signals or barrier semaphores. Data moves between devices by JAX's collectives and lax.ppermute only.
A program may use at most 256 MiB of HBM per device.

```python
import jax
import jax.numpy as jnp
from jax import lax

SLOTS = 16
TILE = 16
STEPS = 2
NTX = 32
NTY = 8
NTZ = 8
NX = 512
NY = 128
NZ = 128


def grain_lists(key):
    key_order = jax.random.fold_in(key, 11)
    key_count = jax.random.fold_in(key, 12)
    key_place = jax.random.fold_in(key, 13)
    key_label = jax.random.fold_in(key, 14)
    coord_x = jnp.arange(NTX)[:, None, None, None]
    coord_y = jnp.arange(NTY)[None, :, None, None]
    coord_z = jnp.arange(NTZ)[None, None, :, None]
    offset = jnp.arange(8)
    owner = (coord_x + offset // 4) % NTX * (NTY * NTZ) + (coord_y + offset // 2 % 2) % NTY * NTZ + (coord_z + offset % 2) % NTZ
    candidates = (owner[..., None] * 2 + jnp.arange(2)).reshape(NTX, NTY, NTZ, 16)
    labels = jax.random.permutation(key_label, 2 * NTX * NTY * NTZ).astype(jnp.int32)
    candidates = labels[candidates]
    scores = jax.random.randint(key_order, (NTX, NTY, NTZ, 16), 0, 2 ** 20) * 16 + jnp.arange(16)
    scores = jnp.where(jnp.arange(16) < 2, jnp.arange(16) - 2, scores)
    order = jnp.argsort(scores, axis=-1, stable=True)
    chosen = jnp.take_along_axis(candidates, order, axis=-1)[..., :SLOTS]
    count = jax.random.randint(key_count, (NTX, NTY, NTZ, 1), SLOTS * 5 // 8, SLOTS)
    listed = jnp.where(jnp.arange(SLOTS) < count, chosen, -1)
    place_scores = jax.random.randint(key_place, (NTX, NTY, NTZ, SLOTS), 0, 2 ** 20) * SLOTS + jnp.arange(SLOTS)
    places = jnp.argsort(place_scores, axis=-1, stable=True)
    return jnp.take_along_axis(listed, places, axis=-1).astype(jnp.int32)


def draw_grain_ids(key, part):
    return grain_lists(key)


def draw_phase_fields(key, part):
    listed = grain_lists(key)
    key = jax.random.fold_in(key, 5)
    values = jax.random.uniform(key, (SLOTS, NX, NY, NZ), jnp.float32)
    active = (listed >= 0).astype(jnp.float32)
    active = jnp.transpose(active, (3, 0, 1, 2))[:, :, None, :, None, :, None]
    shaped = values.reshape(SLOTS, NTX, TILE, NTY, TILE, NTZ, TILE) * active
    return shaped.reshape(SLOTS, NX, NY, NZ).astype(jnp.float32)


def setup_inputs(seed: int = 0) -> dict:
    seeds = jax.random.split(jax.random.key(seed), 3)
    phase_fields = draw_phase_fields(jax.random.fold_in(seeds[2], 71), 0)
    grain_ids = draw_grain_ids(jax.random.fold_in(seeds[2], 71), 0)
    return {"phase_fields": phase_fields, "grain_ids": grain_ids}


TIME_STEP = 0.05
INTERFACE_GAMMA = 1.5
GRADIENT_KAPPA = 0.5


def remap_edge(source, mine, other, axis, step):
    slots, cells_x, cells_y, cells_z = source.shape
    tiles_x, tiles_y, tiles_z, _ = mine.shape
    shaped = source.reshape(slots, tiles_x, cells_x // tiles_x, tiles_y, cells_y // tiles_y, tiles_z, cells_z // tiles_z)
    edge = shaped.shape[2 * axis] - 1 if step > 0 else 0
    match = ((mine[..., :, None] == other[..., None, :]) & (mine[..., :, None] >= 0)).astype(jnp.float32)
    plane = lax.index_in_dim(shaped, edge, 2 * axis, keepdims=True)
    moved = jnp.einsum('abcst,taibjck->saibjck', match, plane, precision=lax.Precision.HIGHEST)
    place = lax.broadcasted_iota(jnp.int32, shaped.shape, 2 * axis) == edge
    return jnp.where(place, moved, shaped).reshape(source.shape)


def update(field, parts):
    laplace = (parts[0] + parts[1]) + (parts[2] + parts[3]) + (parts[4] + parts[5]) - 6.0 * field
    total = jnp.sum(field * field, axis=0)
    square = field * field
    force = square * field - field + 2.0 * INTERFACE_GAMMA * field * (total - square) - GRADIENT_KAPPA * laplace
    return field - TIME_STEP * force


def reference(phase_fields, grain_ids):
    field = phase_fields
    for turn in range(STEPS):
        parts = []
        for axis in (1, 2, 3):
            for step in (-1, 1):
                source = jnp.roll(field, -step, axis)
                other = jnp.roll(grain_ids, -step, axis - 1)
                parts.append(remap_edge(source, grain_ids, other, axis, step))
        field = update(field, parts)
    return field
```

```python
import jax
import jax.numpy as jnp
from jax import lax
from jax.experimental import pallas as pl
from jax.experimental.pallas import tpu as pltpu
from jax.sharding import PartitionSpec as P

SLOTS = 16
TILE = 16
ROWS = TILE * TILE
NZ = 128
NTZ = NZ // TILE
FACE = SLOTS * TILE
HEAD = FACE + 8
RATE = 0.025
HIGHEST = lax.Precision.HIGHEST
F32 = jnp.float32
BF16 = jnp.bfloat16


def iota(shape, dim):
    return lax.broadcasted_iota(jnp.int32, shape, dim)


def sides(axis):
    odd = lax.axis_index(axis) & 1
    return (TILE - 1) * (1 - odd), (TILE - 1) * odd


def flat_ids(ids):
    lane = iota((SLOTS, NZ), 1)
    spread = ((lane & 15) == iota((SLOTS, NZ), 0)).astype(F32)
    wide = jnp.dot(ids.astype(F32), spread, precision=HIGHEST, preferred_element_type=F32)
    own = (iota((NTZ, NZ), 1) >> 4) == iota((NTZ, NZ), 0)
    return jnp.sum(jnp.where(own, wide, 0.0), axis=0, keepdims=True)


def lane_ids(flat):
    pick = jnp.where((iota((SLOTS, NZ), 1) & 15) == iota((SLOTS, NZ), 0), flat, 0.0)
    group = ((iota((NZ, NZ), 0) >> 4) == (iota((NZ, NZ), 1) >> 4)).astype(F32)
    return jnp.dot(pick, group, precision=HIGHEST, preferred_element_type=F32)


def remap(mine, other, plane, match_ref, out_ref, own_ref=None):
    for s in range(SLOTS):
        row = mine[s : s + 1, :]
        match_ref[s] = jnp.where((other == row) & (row >= 0.0), RATE, 0.0)
    for s in range(SLOTS):
        total = None
        if own_ref is not None:
            listed = RATE * jnp.sum(match_ref[s], axis=0, keepdims=True)
            total = listed * own_ref[s * TILE : (s + 1) * TILE, :]
        for t in range(SLOTS):
            term = match_ref[s, t : t + 1, :] * plane[t * TILE : (t + 1) * TILE, :]
            total = term if total is None else total + term
        out_ref[s * TILE : (s + 1) * TILE, :] = total


def take_x(field_ref, x):
    return field_ref[:, pl.ds(pl.multiple_of(x * TILE, TILE), TILE), :].reshape(FACE, NZ)


def take_y(field_ref, s, y):
    return field_ref[s, pl.ds(y, TILE, stride=TILE), :]


def add_faces(field_ref, x_faces, y_faces, xs, ys):
    for ref, x in zip(x_faces, xs):
        at = pl.ds(pl.multiple_of(x * TILE, TILE), TILE)
        field_ref[:, at, :] += ref[...].reshape(SLOTS, TILE, NZ)
    for ref, y in zip(y_faces, ys):
        for s in range(SLOTS):
            at = pl.ds(y, TILE, stride=TILE)
            field_ref[s, at, :] += ref[s * TILE : (s + 1) * TILE, :]


def step(field_ref, ids, out_ref, halves_ref, edge_ref):
    flat = flat_ids(ids)
    mine = lane_ids(flat)
    for s in range(SLOTS):
        value = field_ref[s]
        high = value.astype(BF16)
        halves_ref[s, :, :NZ] = high
        halves_ref[s, :, NZ:] = (value - high.astype(F32)).astype(BF16)
    z, n = iota((2 * NZ, 2 * NZ), 0) & (NZ - 1), iota((2 * NZ, 2 * NZ), 1)
    source = ((n & (NZ - 1)) >> 4) * TILE + jnp.where(n < NZ, TILE - 1, 0)
    at = z == source
    edges = jnp.zeros((ROWS, 2 * NZ), F32)
    for t in range(SLOTS):
        pick = jnp.where(at & ((n & 15) == t), 1.0, 0.0).astype(BF16)
        edges += jnp.dot(halves_ref[t], pick, preferred_element_type=F32)
    high = edges.astype(BF16)
    edge_ref[:, : 2 * NZ] = high
    edge_ref[:, 2 * NZ :] = (edges - high.astype(F32)).astype(BF16)
    r, c = iota((ROWS, ROWS), 0), iota((ROWS, ROWS), 1)
    gap = jnp.abs(r - c)
    beside = (gap == TILE) | ((gap == 1) & ((r >> 4) == (c >> 4)))
    beside = jnp.where(beside, 1.0, 0.0).astype(BF16)
    r, c = iota((2 * NZ, NZ), 0), iota((2 * NZ, NZ), 1)
    rz = r & (NZ - 1)
    along = jnp.where((jnp.abs(rz - c) == 1) & ((rz >> 4) == (c >> 4)), 1.0, 0.0).astype(BF16)
    tile = rz >> 4
    goes = jnp.where(r < NZ, ((tile + 1) & 7) * TILE, ((tile + 7) & 7) * TILE + TILE - 1) == c
    eye = iota((NZ, NZ), 0) == iota((NZ, NZ), 1)
    column = jnp.sum(jnp.where(eye, flat, 0.0), axis=1, keepdims=True)
    column = jnp.concatenate([column, column], axis=0)
    goes = goes & (column >= 0.0)
    total = field_ref[0] * field_ref[0]
    for s in range(1, SLOTS):
        total += field_ref[s] * field_ref[s]
    base = 0.9 - 0.15 * total
    for s in range(SLOTS):
        match = jnp.where(goes & (column == mine[s : s + 1, :]), 1.0, 0.0).astype(BF16)
        near = jnp.dot(halves_ref[s], along, preferred_element_type=F32)
        near += jnp.dot(
            edge_ref[...], jnp.concatenate([match, match], axis=0), preferred_element_type=F32
        )
        plane = jnp.dot(beside, halves_ref[s], preferred_element_type=F32)
        near += plane[:, :NZ] + plane[:, NZ:]
        value = field_ref[s]
        out_ref[s] = value * (base + 0.1 * (value * value)) + RATE * near


def pack_kernel(field_ref, ids_ref, ya_ref, yb_ref, xa_ref, xb_ref):
    flat = flat_ids(ids_ref[...])
    for refs, axis in (((ya_ref, yb_ref), "gy"), ((xa_ref, xb_ref), "gx")):
        for ref, side in zip(refs, sides(axis)):
            if axis == "gx":
                ref[:FACE, :] = take_x(field_ref, side)
            else:
                for s in range(SLOTS):
                    ref[s * TILE : (s + 1) * TILE, :] = take_y(field_ref, s, side)
            ref[FACE:, :] = jnp.broadcast_to(flat, (HEAD - FACE, NZ))


def first_kernel(field_ref, ids_ref, out_ref, ya_ref, yb_ref, xa_ref, xb_ref, halves_ref, edge_ref):
    step(field_ref, ids_ref[...], out_ref, halves_ref, edge_ref)
    for ref, side in zip((xa_ref, xb_ref), sides("gx")):
        ref[...] = take_x(out_ref, side)
    for ref, side in zip((ya_ref, yb_ref), sides("gy")):
        for s in range(SLOTS):
            ref[s * TILE : (s + 1) * TILE, :] = take_y(out_ref, s, side)


def add_corners(out_refs, out_sides, add_refs, add_sides):
    for out_ref, here in zip(out_refs, out_sides):
        for add_ref, there in zip(add_refs, add_sides):
            at = pl.ds(there, SLOTS, stride=TILE)
            out_ref[at, :] += add_ref[pl.ds(here, SLOTS, stride=TILE), :]


def x_kernel(ids_ref, ga_ref, gb_ref, ya_ref, yb_ref, ya_out, yb_out, ca_ref, cb_ref, match_ref):
    mine = lane_ids(flat_ids(ids_ref[...]))
    for got, out in ((ga_ref, ca_ref), (gb_ref, cb_ref)):
        remap(mine, lane_ids(got[FACE : FACE + 1, :]), got, match_ref, out)
    ya_out[...] = ya_ref[...]
    yb_out[...] = yb_ref[...]
    add_corners((ya_out, yb_out), sides("gy"), (ca_ref, cb_ref), sides("gx"))


def y_kernel(ids_ref, ga_ref, gb_ref, xa_ref, xb_ref, cxa_ref, cxb_ref, xa_out, xb_out, ca_ref, cb_ref, match_ref):
    mine = lane_ids(flat_ids(ids_ref[...]))
    for got, out in ((ga_ref, ca_ref), (gb_ref, cb_ref)):
        remap(mine, lane_ids(got[FACE : FACE + 1, :]), got, match_ref, out)
    xa_out[...] = xa_ref[...] + cxa_ref[...]
    xb_out[...] = xb_ref[...] + cxb_ref[...]
    add_corners((xa_out, xb_out), sides("gx"), (ca_ref, cb_ref), sides("gy"))


def second_kernel(field_ref, ids_ref, xa_ref, xb_ref, ya_ref, yb_ref, out_ref, state_ref, halves_ref, edge_ref):
    state_ref[...] = field_ref[...]
    add_faces(state_ref, (xa_ref, xb_ref), (ya_ref, yb_ref), sides("gx"), sides("gy"))
    step(state_ref, ids_ref[...], out_ref, halves_ref, edge_ref)


def last_kernel(
    part_ref, ids_ref, xa_ref, xb_ref, ya_ref, yb_ref, hxa_ref, hxb_ref, hya_ref, hyb_ref, oya_ref, oyb_ref,
    out_ref, match_ref, cxa_ref, cxb_ref, cya_ref, cyb_ref,
):
    mine = lane_ids(flat_ids(ids_ref[...]))
    out_ref[...] = part_ref[...]
    for got, head, out, own in (
        (xa_ref, hxa_ref, cxa_ref, None),
        (xb_ref, hxb_ref, cxb_ref, None),
        (ya_ref, hya_ref, cya_ref, oya_ref),
        (yb_ref, hyb_ref, cyb_ref, oyb_ref),
    ):
        remap(mine, lane_ids(head[FACE : FACE + 1, :]), got, match_ref, out, own)
    add_faces(out_ref, (cxa_ref, cxb_ref), (cya_ref, cyb_ref), sides("gx"), sides("gy"))


def call(body, outs, scratch=(), flops=0, bytes_accessed=0):
    return pl.pallas_call(
        body,
        out_shape=[jax.ShapeDtypeStruct(shape, F32) for shape in outs],
        scratch_shapes=[pltpu.VMEM(shape, dtype) for shape, dtype in scratch],
        compiler_params=pltpu.CompilerParams(vmem_limit_bytes=40 * 2**20),
        cost_estimate=pl.CostEstimate(
            flops=flops, bytes_accessed=bytes_accessed, transcendentals=0
        ),
    )


def pairs(count, start):
    order = []
    for i in range(start, start + count, 2):
        a, b = i % count, (i + 1) % count
        order += [(a, b), (b, a)]
    return order


def exchange(value, axis, which):
    return lax.ppermute(value, axis, pairs(lax.axis_size(axis), which))


WHOLE = (SLOTS, ROWS, NZ)
SIDE = (FACE, NZ)
FIRST = (HEAD, NZ)
STEP_SCRATCH = [((SLOTS, ROWS, 2 * NZ), BF16), ((ROWS, 4 * NZ), BF16)]
MATCH = ((SLOTS, SLOTS, NZ), F32)


def shards(phase_fields, grain_ids):
    field = phase_fields.reshape(WHOLE)
    ids = grain_ids.reshape(NTZ, SLOTS)
    sya, syb, sxa, sxb = call(pack_kernel, [FIRST] * 4, bytes_accessed=3 << 20)(field, ids)
    gya, gyb = exchange(sya, "gy", 0), exchange(syb, "gy", 1)
    gxa, gxb = exchange(sxa, "gx", 0), exchange(sxb, "gx", 1)
    part, pya, pyb, pxa, pxb = call(
        first_kernel, [WHOLE] + [SIDE] * 4, STEP_SCRATCH, flops=4 << 30, bytes_accessed=4 << 20
    )(field, ids)
    pya, pyb, cxa, cxb = call(x_kernel, [SIDE] * 4, [MATCH], bytes_accessed=1 << 20)(
        ids, gxa, gxb, pya, pyb
    )
    gpya, gpyb = exchange(pya, "gy", 0), exchange(pyb, "gy", 1)
    pxa, pxb, cya, cyb = call(y_kernel, [SIDE] * 4, [MATCH], bytes_accessed=1 << 20)(
        ids, gya, gyb, pxa, pxb, cxa, cxb
    )
    gpxa, gpxb = exchange(pxa, "gx", 0), exchange(pxb, "gx", 1)
    (part,) = call(
        second_kernel, [WHOLE], [(WHOLE, F32)] + STEP_SCRATCH, flops=4 << 30, bytes_accessed=5 << 20
    )(part, ids, cxa, cxb, cya, cyb)
    (out,) = call(last_kernel, [WHOLE], [MATCH] + [(SIDE, F32)] * 4, bytes_accessed=5 << 20)(
        part, ids, gpxa, gpxb, gpya, gpyb, gxa, gxb, gya, gyb, sya, syb
    )
    return out.reshape(phase_fields.shape)


def solution(mesh):
    in_specs = (P(None, "gx", "gy", None), P("gx", "gy", None, None))
    out_specs = P(None, "gx", "gy", None)
    return jax.shard_map(shards, mesh=mesh, in_specs=in_specs, out_specs=out_specs, check_vma=False)
```

```python
import jax
import jax.numpy as jnp
from jax import lax
from jax.experimental import pallas as pl
from jax.experimental.pallas import tpu as pltpu
from jax.sharding import PartitionSpec as P

SLOTS = 16
TILE = 16
ROWS = TILE * TILE
NZ = 128
NTZ = NZ // TILE
FACE = SLOTS * TILE
SENT = SLOTS - 1
PART = SENT * TILE
HEAD = PART + 8
RATE = 0.025
HIGHEST = lax.Precision.HIGHEST
F32 = jnp.float32
BF16 = jnp.bfloat16


def iota(shape, dim):
    return lax.broadcasted_iota(jnp.int32, shape, dim)


def sides(axis):
    odd = lax.axis_index(axis) & 1
    return (TILE - 1) * (1 - odd), (TILE - 1) * odd


def flat_ids(ids):
    lane = iota((SLOTS, NZ), 1)
    spread = ((lane & 15) == iota((SLOTS, NZ), 0)).astype(F32)
    wide = jnp.dot(ids.astype(F32), spread, precision=HIGHEST, preferred_element_type=F32)
    own = (iota((NTZ, NZ), 1) >> 4) == iota((NTZ, NZ), 0)
    return jnp.sum(jnp.where(own, wide, 0.0), axis=0, keepdims=True)


def lane_ids(flat):
    pick = jnp.where((iota((SLOTS, NZ), 1) & 15) == iota((SLOTS, NZ), 0), flat, 0.0)
    group = ((iota((NZ, NZ), 0) >> 4) == (iota((NZ, NZ), 1) >> 4)).astype(F32)
    return jnp.dot(pick, group, precision=HIGHEST, preferred_element_type=F32)


def kept(mine):
    rows = []
    for s in range(SENT):
        row = jnp.where(mine[s : s + 1, :] >= 0.0, 1.0, 0.0)
        rows.append(row * rows[-1] if rows else row)
    return rows


def sent_ids(ids):
    rows = [
        jnp.where(row > 0.0, ids[s : s + 1, :], ids[s + 1 : s + 2, :])
        for s, row in enumerate(kept(ids))
    ]
    return jnp.concatenate(rows + [jnp.full((1, NZ), -2.0, F32)], axis=0)


def send(face_ref, mine, out_ref):
    for s, row in enumerate(kept(mine)):
        keep = jnp.broadcast_to(row, (TILE, NZ)) > 0.0
        here, after = (face_ref[t * TILE : (t + 1) * TILE, :] for t in (s, s + 1))
        out_ref[s * TILE : (s + 1) * TILE, :] = jnp.where(keep, here, after)


def matches(mine, other, match_ref):
    for s in range(SLOTS):
        row = mine[s : s + 1, :]
        match_ref[s] = jnp.where((other == row) & (row >= 0.0), RATE, 0.0)


def remap(plane, match_ref, out_ref, own_ref=None, count=SENT):
    for s in range(SLOTS):
        total = None
        if own_ref is not None:
            listed = RATE * jnp.sum(match_ref[s], axis=0, keepdims=True)
            total = listed * own_ref[s * TILE : (s + 1) * TILE, :]
        for t in range(count):
            term = match_ref[s, t : t + 1, :] * plane[t * TILE : (t + 1) * TILE, :]
            total = term if total is None else total + term
        out_ref[s * TILE : (s + 1) * TILE, :] = total


def take_x(field_ref, x):
    return field_ref[:, pl.ds(pl.multiple_of(x * TILE, TILE), TILE), :].reshape(FACE, NZ)


def take_y(field_ref, s, y):
    return field_ref[s, pl.ds(y, TILE, stride=TILE), :]


def add_faces(field_ref, x_faces, y_faces, xs, ys):
    for ref, x in zip(x_faces, xs):
        at = pl.ds(pl.multiple_of(x * TILE, TILE), TILE)
        field_ref[:, at, :] += ref[...].reshape(SLOTS, TILE, NZ)
    for ref, y in zip(y_faces, ys):
        for s in range(SLOTS):
            at = pl.ds(y, TILE, stride=TILE)
            field_ref[s, at, :] += ref[s * TILE : (s + 1) * TILE, :]


def step(field_ref, lists_ref, out_ref, halves_ref, edge_ref):
    flat = lists_ref[SLOTS : SLOTS + 1, :]
    for s in range(SLOTS):
        value = field_ref[s]
        high = value.astype(BF16)
        halves_ref[s, :, :NZ] = high
        halves_ref[s, :, NZ:] = (value - high.astype(F32)).astype(BF16)
    r, c = iota((2 * NZ, 2 * NZ), 0), iota((2 * NZ, 2 * NZ), 1)
    rz, cz = r & (NZ - 1), c & (NZ - 1)
    at = rz == (cz >> 4) * TILE + jnp.where(c < NZ, TILE - 1, 0)
    edges = jnp.zeros((ROWS, 2 * NZ), F32)
    for t in range(SLOTS):
        pick = jnp.where(at & ((c & 15) == t), 1.0, 0.0).astype(BF16)
        edges += jnp.dot(halves_ref[t], pick, preferred_element_type=F32)
    high = edges.astype(BF16)
    edge_ref[:, : 2 * NZ] = high
    edge_ref[:, 2 * NZ :] = (edges - high.astype(F32)).astype(BF16)
    eye = iota((NZ, NZ), 0) == iota((NZ, NZ), 1)
    column = jnp.sum(jnp.where(eye, flat, 0.0), axis=1, keepdims=True)
    column = jnp.concatenate([column, column], axis=0)
    row = jnp.concatenate([flat, flat], axis=1)
    hop = ((r >> 7) == (c >> 7)) & ((cz >> 4) == (((rz >> 4) + jnp.where(r < NZ, 1, 7)) & 7))
    match = jnp.where(hop & (column == row) & (column >= 0.0), 1.0, 0.0).astype(BF16)
    moved = jnp.dot(edge_ref[:, : 2 * NZ], match, preferred_element_type=F32)
    moved += jnp.dot(edge_ref[:, 2 * NZ :], match, preferred_element_type=F32)
    below, above = moved[:, :NZ], moved[:, NZ:]
    gap = jnp.abs(r - c)
    beside = (gap == TILE) | ((gap == 1) & ((r >> 4) == (c >> 4)))
    beside = jnp.where(beside, 1.0, 0.0).astype(BF16)
    r, c = iota((2 * NZ, NZ), 0) & (NZ - 1), iota((2 * NZ, NZ), 1)
    along = jnp.where((jnp.abs(r - c) == 1) & ((r >> 4) == (c >> 4)), 1.0, 0.0).astype(BF16)
    total = field_ref[0] * field_ref[0]
    for s in range(1, SLOTS):
        total += field_ref[s] * field_ref[s]
    base = 0.9 - 0.15 * total
    lane = iota((ROWS, NZ), 1) & 15
    for s in range(SLOTS):
        low = turn(below, -s)
        near = jnp.where(lane == 0, low, jnp.where(lane == TILE - 1, turn(above, TILE - 1 - s), 0.0))
        near += jnp.dot(halves_ref[s], along, preferred_element_type=F32)
        plane = jnp.dot(beside, halves_ref[s], preferred_element_type=F32)
        near += plane[:, :NZ] + plane[:, NZ:]
        value = field_ref[s]
        out_ref[s] = value * (base + 0.1 * (value * value)) + RATE * near


def turn(value, by, dim=1):
    by %= value.shape[dim]
    return pltpu.roll(value, by, dim) if by else value


def pack_kernel(
    field_ref, ids_ref, xa_ref, xb_ref, ya_ref, yb_ref, planes_ref, rows_ref, ids_vmem, face_ref, sems
):
    ids = pltpu.make_async_copy(ids_ref, ids_vmem, sems.at[4])
    planes = [
        pltpu.make_async_copy(field_ref.at[:, pl.ds(x, 1), :, :], planes_ref.at[i], sems.at[i])
        for i, x in enumerate((0, TILE - 1))
    ]
    rows = [
        pltpu.make_async_copy(field_ref.at[:, :, pl.ds(y, 1), :], rows_ref.at[i], sems.at[2 + i])
        for i, y in enumerate((0, TILE - 1))
    ]
    for copy in [ids] + planes + rows:
        copy.start()
    ids.wait()
    flat = flat_ids(ids_vmem[...])
    mine = lane_ids(flat)
    flat = jnp.broadcast_to(flat, (HEAD - PART, NZ))
    for copies, from_ref, refs, axis in (
        (planes, planes_ref, (xa_ref, xb_ref), "gx"),
        (rows, rows_ref, (ya_ref, yb_ref), "gy"),
    ):
        odd = lax.axis_index(axis) & 1
        for copy in copies:
            copy.wait()
        for n, ref in enumerate(refs):
            face_ref[...] = from_ref[(odd + 1 + n) % 2].reshape(FACE, NZ)
            send(face_ref, mine, ref)
            ref[PART:, :] = flat


def take_faces(field_ref, x_refs, y_refs):
    for ref, side in zip(x_refs, sides("gx")):
        ref[...] = take_x(field_ref, side)
    for ref, side in zip(y_refs, sides("gy")):
        for s in range(SLOTS):
            ref[s * TILE : (s + 1) * TILE, :] = take_y(field_ref, s, side)


def first_kernel(
    field_ref, ids_ref, out_ref, xa_ref, xb_ref, ya_ref, yb_ref, oya_ref, oyb_ref, lists_ref, halves_ref, edge_ref
):
    flat = flat_ids(ids_ref[...])
    lists_ref[:SLOTS, :] = lane_ids(flat)
    lists_ref[SLOTS:, :] = jnp.broadcast_to(flat, (8, NZ))
    step(field_ref, lists_ref, out_ref, halves_ref, edge_ref)
    take_faces(field_ref, (), (oya_ref, oyb_ref))
    take_faces(out_ref, (xa_ref, xb_ref), (ya_ref, yb_ref))


def arrive(lists_ref, gots, matchs, outs):
    for got, match, out in zip(gots, matchs, outs):
        matches(lists_ref[:SLOTS, :], sent_ids(lane_ids(got[PART : PART + 1, :])), match)
        remap(got, match, out)


def add_rows(out_ref, place, add_refs, add_places):
    for ref, there in zip(add_refs, add_places):
        out_ref[pl.ds(there, SLOTS, stride=TILE), :] += ref[pl.ds(place, SLOTS, stride=TILE), :]


def x_kernel(lists_ref, ga_ref, gb_ref, ya_ref, yb_ref, ya_out, yb_out, ca_ref, cb_ref, ma_ref, mb_ref, face_ref):
    arrive(lists_ref, (ga_ref, gb_ref), (ma_ref, mb_ref), (ca_ref, cb_ref))
    for out, part, y in zip((ya_out, yb_out), (ya_ref, yb_ref), sides("gy")):
        face_ref[...] = part[...]
        add_rows(face_ref, y, (ca_ref, cb_ref), sides("gx"))
        send(face_ref, lists_ref[:SLOTS, :], out)


def y_kernel(
    lists_ref, ga_ref, gb_ref, xa_ref, xb_ref, cxa_ref, cxb_ref,
    xa_out, xb_out, ca_ref, cb_ref, ma_ref, mb_ref, face_ref,
):
    arrive(lists_ref, (ga_ref, gb_ref), (ma_ref, mb_ref), (ca_ref, cb_ref))
    for out, part, add, x in zip((xa_out, xb_out), (xa_ref, xb_ref), (cxa_ref, cxb_ref), sides("gx")):
        face_ref[...] = part[...] + add[...]
        add_rows(face_ref, x, (ca_ref, cb_ref), sides("gy"))
        send(face_ref, lists_ref[:SLOTS, :], out)


def second_kernel(
    field_ref, lists_ref, cxa_ref, cxb_ref, cya_ref, cyb_ref,
    out_ref, xa_ref, xb_ref, ya_ref, yb_ref, state_ref, halves_ref, edge_ref,
):
    state_ref[...] = field_ref[...]
    add_faces(state_ref, (cxa_ref, cxb_ref), (cya_ref, cyb_ref), sides("gx"), sides("gy"))
    step(state_ref, lists_ref, out_ref, halves_ref, edge_ref)
    take_faces(out_ref, (xa_ref, xb_ref), (ya_ref, yb_ref))


def last_kernel(
    part_ref, gxa_ref, gxb_ref, gya_ref, gyb_ref, mxa_ref, mxb_ref, mya_ref, myb_ref, oya_ref, oyb_ref,
    fxa_ref, fxb_ref, fya_ref, fyb_ref, out_ref, cxa_ref, cxb_ref, face_ref, planes_ref, rows_ref, sems,
):
    del part_ref
    odd = lax.axis_index("gx") & 1
    for n, (got, match, face, out) in enumerate(
        ((gxa_ref, mxa_ref, fxa_ref, cxa_ref), (gxb_ref, mxb_ref, fxb_ref, cxb_ref))
    ):
        remap(got, match, out)
        planes_ref[(odd + 1 + n) % 2] = (out[...] + face[...]).reshape(SLOTS, 1, TILE, NZ)
    planes = [
        pltpu.make_async_copy(planes_ref.at[i], out_ref.at[:, pl.ds(x, 1), :, :], sems.at[i])
        for i, x in enumerate((0, TILE - 1))
    ]
    for copy in planes:
        copy.start()
    odd = lax.axis_index("gy") & 1
    for n, (got, match, own, face, y) in enumerate(zip(
        (gya_ref, gyb_ref), (mya_ref, myb_ref), (oya_ref, oyb_ref), (fya_ref, fyb_ref), sides("gy")
    )):
        remap(got, match, face_ref, own)
        add_rows(face_ref, y, (cxa_ref, cxb_ref), sides("gx"))
        rows_ref[(odd + 1 + n) % 2] = (face_ref[...] + face[...]).reshape(SLOTS, TILE, 1, NZ)
    for copy in planes:
        copy.wait()
    rows = [
        pltpu.make_async_copy(rows_ref.at[i], out_ref.at[:, :, pl.ds(y, 1), :], sems.at[2 + i])
        for i, y in enumerate((0, TILE - 1))
    ]
    for copy in rows:
        copy.start()
    for copy in rows:
        copy.wait()


def call(body, outs, scratch=(), flops=0, bytes_accessed=0, vmem=40, **specs):
    return pl.pallas_call(
        body,
        out_shape=[jax.ShapeDtypeStruct(shape, F32) for shape in outs],
        scratch_shapes=[pltpu.VMEM(*one) if isinstance(one, tuple) else one for one in scratch],
        compiler_params=pltpu.CompilerParams(vmem_limit_bytes=vmem * 2**20),
        cost_estimate=pl.CostEstimate(
            flops=flops, bytes_accessed=bytes_accessed, transcendentals=0
        ),
        **specs,
    )


def pairs(count, start):
    order = []
    for i in range(start, start + count, 2):
        a, b = i % count, (i + 1) % count
        order += [(a, b), (b, a)]
    return order


def exchange(value, axis, which):
    return lax.ppermute(value, axis, pairs(lax.axis_size(axis), which))


WHOLE = (SLOTS, ROWS, NZ)
SIDE = (FACE, NZ)
FIRST = (HEAD, NZ)
SECOND = (PART, NZ)
LISTS = (SLOTS + 8, NZ)
STEP_SCRATCH = [((SLOTS, ROWS, 2 * NZ), BF16), ((ROWS, 4 * NZ), BF16)]
MATCH = (SLOTS, SLOTS, NZ)
ANYWHERE = pl.BlockSpec(memory_space=pl.ANY)
HERE = pl.BlockSpec(memory_space=pltpu.VMEM)


def shards(phase_fields, grain_ids):
    field = phase_fields.reshape(WHOLE)
    ids = grain_ids.reshape(NTZ, SLOTS)
    sxa, sxb, sya, syb = call(
        pack_kernel,
        [FIRST] * 4,
        [
            ((2, SLOTS, 1, TILE, NZ), F32),
            ((2, SLOTS, TILE, 1, NZ), F32),
            ((NTZ, SLOTS), jnp.int32),
            (SIDE, F32),
            pltpu.SemaphoreType.DMA((5,)),
        ],
        bytes_accessed=3 << 20,
        vmem=62,
        in_specs=[ANYWHERE, ANYWHERE],
    )(phase_fields, ids)
    gxa, gxb = exchange(sxa, "gx", 0), exchange(sxb, "gx", 1)
    gya, gyb = exchange(sya, "gy", 0), exchange(syb, "gy", 1)
    part, pxa, pxb, pya, pyb, oya, oyb, lists = call(
        first_kernel,
        [WHOLE] + [SIDE] * 6 + [LISTS],
        STEP_SCRATCH,
        flops=4 << 30,
        bytes_accessed=4 << 20,
    )(field, ids)
    tya, tyb, cxa, cxb, mxa, mxb = call(
        x_kernel, [SECOND] * 2 + [SIDE] * 2 + [MATCH] * 2, [(SIDE, F32)], bytes_accessed=1 << 20
    )(lists, gxa, gxb, pya, pyb)
    gpya, gpyb = exchange(tya, "gy", 0), exchange(tyb, "gy", 1)
    txa, txb, cya, cyb, mya, myb = call(
        y_kernel, [SECOND] * 2 + [SIDE] * 2 + [MATCH] * 2, [(SIDE, F32)], bytes_accessed=1 << 20
    )(lists, gya, gyb, pxa, pxb, cxa, cxb)
    gpxa, gpxb = exchange(txa, "gx", 0), exchange(txb, "gx", 1)
    part, fxa, fxb, fya, fyb = call(
        second_kernel,
        [WHOLE] + [SIDE] * 4,
        [(WHOLE, F32)] + STEP_SCRATCH,
        flops=4 << 30,
        bytes_accessed=5 << 20,
    )(part, lists, cxa, cxb, cya, cyb)
    (out,) = call(
        last_kernel,
        [phase_fields.shape],
        [
            (SIDE, F32),
            (SIDE, F32),
            (SIDE, F32),
            ((2, SLOTS, 1, TILE, NZ), F32),
            ((2, SLOTS, TILE, 1, NZ), F32),
            pltpu.SemaphoreType.DMA((4,)),
        ],
        bytes_accessed=5 << 20,
        in_specs=[ANYWHERE] + [HERE] * 14,
        out_specs=[ANYWHERE],
        input_output_aliases={0: 0},
    )(
        part.reshape(phase_fields.shape), gpxa, gpxb, gpya, gpyb, mxa, mxb, mya, myb, oya, oyb, fxa, fxb, fya, fyb
    )
    return out


def solution(mesh):
    in_specs = (P(None, "gx", "gy", None), P("gx", "gy", None, None))
    out_specs = P(None, "gx", "gy", None)
    return jax.shard_map(shards, mesh=mesh, in_specs=in_specs, out_specs=out_specs, check_vma=False)
```

```python
import jax
import jax.numpy as jnp
from jax import lax
from jax.experimental import pallas as pl
from jax.experimental.pallas import tpu as pltpu
from jax.sharding import PartitionSpec as P

SLOTS = 16
TILE = 16
ROWS = TILE * TILE
NZ = 128
NTZ = NZ // TILE
FACE = SLOTS * TILE
SENT = SLOTS - 1
PART = SENT * TILE
HEAD = PART + 8
RATE = 0.025
HIGHEST = lax.Precision.HIGHEST
F32 = jnp.float32
BF16 = jnp.bfloat16


def iota(shape, dim):
    return lax.broadcasted_iota(jnp.int32, shape, dim)


def sides(axis):
    odd = lax.axis_index(axis) & 1
    return (TILE - 1) * (1 - odd), (TILE - 1) * odd


def flat_ids(ids):
    lane = iota((SLOTS, NZ), 1)
    spread = ((lane & 15) == iota((SLOTS, NZ), 0)).astype(F32)
    wide = jnp.dot(ids.astype(F32), spread, precision=HIGHEST, preferred_element_type=F32)
    own = (iota((NTZ, NZ), 1) >> 4) == iota((NTZ, NZ), 0)
    return jnp.sum(jnp.where(own, wide, 0.0), axis=0, keepdims=True)


def lane_ids(flat):
    pick = jnp.where((iota((SLOTS, NZ), 1) & 15) == iota((SLOTS, NZ), 0), flat, 0.0)
    group = ((iota((NZ, NZ), 0) >> 4) == (iota((NZ, NZ), 1) >> 4)).astype(F32)
    return jnp.dot(pick, group, precision=HIGHEST, preferred_element_type=F32)


def kept(mine):
    rows = []
    for s in range(SENT):
        row = jnp.where(mine[s : s + 1, :] >= 0.0, 1.0, 0.0)
        rows.append(row * rows[-1] if rows else row)
    return rows


def sent_ids(ids):
    rows = [
        jnp.where(row > 0.0, ids[s : s + 1, :], ids[s + 1 : s + 2, :])
        for s, row in enumerate(kept(ids))
    ]
    return jnp.concatenate(rows + [jnp.full((1, NZ), -2.0, F32)], axis=0)


def send(face_ref, mine, out_ref):
    for s, row in enumerate(kept(mine)):
        keep = jnp.broadcast_to(row, (TILE, NZ)) > 0.0
        here, after = (face_ref[t * TILE : (t + 1) * TILE, :] for t in (s, s + 1))
        out_ref[s * TILE : (s + 1) * TILE, :] = jnp.where(keep, here, after)


def matches(mine, other, match_ref):
    for s in range(SLOTS):
        row = mine[s : s + 1, :]
        match_ref[s] = jnp.where((other == row) & (row >= 0.0), RATE, 0.0)


def remap(plane, match_ref, out_ref, own_ref=None, count=SENT):
    for s in range(SLOTS):
        total = None
        if own_ref is not None:
            listed = RATE * jnp.sum(match_ref[s], axis=0, keepdims=True)
            total = listed * own_ref[s * TILE : (s + 1) * TILE, :]
        for t in range(count):
            term = match_ref[s, t : t + 1, :] * plane[t * TILE : (t + 1) * TILE, :]
            total = term if total is None else total + term
        out_ref[s * TILE : (s + 1) * TILE, :] = total


def take_x(field_ref, x):
    return field_ref[:, pl.ds(pl.multiple_of(x * TILE, TILE), TILE), :].reshape(FACE, NZ)


def take_y(field_ref, s, y):
    return field_ref[s, pl.ds(y, TILE, stride=TILE), :]


def add_faces(field_ref, x_faces, y_faces, xs, ys):
    for ref, x in zip(x_faces, xs):
        at = pl.ds(pl.multiple_of(x * TILE, TILE), TILE)
        field_ref[:, at, :] += ref[...].reshape(SLOTS, TILE, NZ)
    for ref, y in zip(y_faces, ys):
        for s in range(SLOTS):
            at = pl.ds(y, TILE, stride=TILE)
            field_ref[s, at, :] += ref[s * TILE : (s + 1) * TILE, :]


def step(field_ref, lists_ref, out_ref, halves_ref, edge_ref):
    flat = lists_ref[SLOTS : SLOTS + 1, :]
    for s in range(SLOTS):
        value = field_ref[s]
        high = value.astype(BF16)
        halves_ref[s, :, :NZ] = high
        halves_ref[s, :, NZ:] = (value - high.astype(F32)).astype(BF16)
    r, c = iota((2 * NZ, 2 * NZ), 0), iota((2 * NZ, 2 * NZ), 1)
    rz, cz = r & (NZ - 1), c & (NZ - 1)
    at = rz == (cz >> 4) * TILE + jnp.where(c < NZ, TILE - 1, 0)
    edges = jnp.zeros((ROWS, 2 * NZ), F32)
    for t in range(SLOTS):
        pick = jnp.where(at & ((c & 15) == t), 1.0, 0.0).astype(BF16)
        edges += jnp.dot(halves_ref[t], pick, preferred_element_type=F32)
    high = edges.astype(BF16)
    edge_ref[:, : 2 * NZ] = high
    edge_ref[:, 2 * NZ :] = (edges - high.astype(F32)).astype(BF16)
    eye = iota((NZ, NZ), 0) == iota((NZ, NZ), 1)
    column = jnp.sum(jnp.where(eye, flat, 0.0), axis=1, keepdims=True)
    column = jnp.concatenate([column, column], axis=0)
    row = jnp.concatenate([flat, flat], axis=1)
    hop = ((r >> 7) == (c >> 7)) & ((cz >> 4) == (((rz >> 4) + jnp.where(r < NZ, 1, 7)) & 7))
    match = jnp.where(hop & (column == row) & (column >= 0.0), 1.0, 0.0).astype(BF16)
    moved = jnp.dot(edge_ref[:, : 2 * NZ], match, preferred_element_type=F32)
    moved += jnp.dot(edge_ref[:, 2 * NZ :], match, preferred_element_type=F32)
    below, above = moved[:, :NZ], moved[:, NZ:]
    gap = jnp.abs(r - c)
    beside = (gap == TILE) | ((gap == 1) & ((r >> 4) == (c >> 4)))
    beside = jnp.where(beside, 1.0, 0.0).astype(BF16)
    r, c = iota((2 * NZ, NZ), 0) & (NZ - 1), iota((2 * NZ, NZ), 1)
    along = jnp.where((jnp.abs(r - c) == 1) & ((r >> 4) == (c >> 4)), 1.0, 0.0).astype(BF16)
    total = field_ref[0] * field_ref[0]
    for s in range(1, SLOTS):
        total += field_ref[s] * field_ref[s]
    base = 0.9 - 0.15 * total
    lane = iota((ROWS, NZ), 1) & 15
    for s in range(SLOTS):
        low = turn(below, -s)
        near = jnp.where(lane == 0, low, jnp.where(lane == TILE - 1, turn(above, TILE - 1 - s), 0.0))
        near += jnp.dot(halves_ref[s], along, preferred_element_type=F32)
        plane = jnp.dot(beside, halves_ref[s], preferred_element_type=F32)
        near += plane[:, :NZ] + plane[:, NZ:]
        value = field_ref[s]
        out_ref[s] = value * (base + 0.1 * (value * value)) + RATE * near


def turn(value, by, dim=1):
    by %= value.shape[dim]
    return pltpu.roll(value, by, dim) if by else value


def pack_kernel(
    field_ref, ids_ref, xa_ref, xb_ref, ya_ref, yb_ref, planes_ref, rows_ref, ids_vmem, face_ref, sems
):
    ids = pltpu.make_async_copy(ids_ref, ids_vmem, sems.at[4])
    planes = [
        pltpu.make_async_copy(field_ref.at[:, pl.ds(x, 1), :, :], planes_ref.at[i], sems.at[i])
        for i, x in enumerate((0, TILE - 1))
    ]
    rows = [
        pltpu.make_async_copy(field_ref.at[:, :, pl.ds(y, 1), :], rows_ref.at[i], sems.at[2 + i])
        for i, y in enumerate((0, TILE - 1))
    ]
    for copy in [ids] + planes + rows:
        copy.start()
    ids.wait()
    flat = flat_ids(ids_vmem[...])
    mine = lane_ids(flat)
    flat = jnp.broadcast_to(flat, (HEAD - PART, NZ))
    for copies, from_ref, refs, axis in (
        (planes, planes_ref, (xa_ref, xb_ref), "gx"),
        (rows, rows_ref, (ya_ref, yb_ref), "gy"),
    ):
        odd = lax.axis_index(axis) & 1
        for copy in copies:
            copy.wait()
        for n, ref in enumerate(refs):
            face_ref[...] = from_ref[(odd + 1 + n) % 2].reshape(FACE, NZ)
            send(face_ref, mine, ref)
            ref[PART:, :] = flat


def take_faces(field_ref, x_refs, y_refs):
    for ref, side in zip(x_refs, sides("gx")):
        ref[...] = take_x(field_ref, side)
    for ref, side in zip(y_refs, sides("gy")):
        for s in range(SLOTS):
            ref[s * TILE : (s + 1) * TILE, :] = take_y(field_ref, s, side)


def first_kernel(
    field_ref, ids_ref, out_ref, xa_ref, xb_ref, ya_ref, yb_ref, oya_ref, oyb_ref, lists_ref, halves_ref, edge_ref
):
    flat = flat_ids(ids_ref[...])
    lists_ref[:SLOTS, :] = lane_ids(flat)
    lists_ref[SLOTS:, :] = jnp.broadcast_to(flat, (8, NZ))
    step(field_ref, lists_ref, out_ref, halves_ref, edge_ref)
    take_faces(field_ref, (), (oya_ref, oyb_ref))
    take_faces(out_ref, (xa_ref, xb_ref), (ya_ref, yb_ref))


def arrive(lists_ref, gots, matchs, outs):
    for got, match, out in zip(gots, matchs, outs):
        matches(lists_ref[:SLOTS, :], sent_ids(lane_ids(got[PART : PART + 1, :])), match)
        remap(got, match, out)


def add_rows(out_ref, place, add_refs, add_places):
    for ref, there in zip(add_refs, add_places):
        out_ref[pl.ds(there, SLOTS, stride=TILE), :] += ref[pl.ds(place, SLOTS, stride=TILE), :]


def x_kernel(lists_ref, ga_ref, gb_ref, ya_ref, yb_ref, ya_out, yb_out, ca_ref, cb_ref, ma_ref, mb_ref, face_ref):
    arrive(lists_ref, (ga_ref, gb_ref), (ma_ref, mb_ref), (ca_ref, cb_ref))
    for out, part, y in zip((ya_out, yb_out), (ya_ref, yb_ref), sides("gy")):
        face_ref[...] = part[...]
        add_rows(face_ref, y, (ca_ref, cb_ref), sides("gx"))
        send(face_ref, lists_ref[:SLOTS, :], out)


def y_kernel(
    lists_ref, ga_ref, gb_ref, xa_ref, xb_ref, cxa_ref, cxb_ref,
    xa_out, xb_out, ca_ref, cb_ref, ma_ref, mb_ref, face_ref,
):
    arrive(lists_ref, (ga_ref, gb_ref), (ma_ref, mb_ref), (ca_ref, cb_ref))
    for out, part, add, x in zip((xa_out, xb_out), (xa_ref, xb_ref), (cxa_ref, cxb_ref), sides("gx")):
        face_ref[...] = part[...] + add[...]
        add_rows(face_ref, x, (ca_ref, cb_ref), sides("gy"))
        send(face_ref, lists_ref[:SLOTS, :], out)


def second_kernel(
    field_ref, lists_ref, cxa_ref, cxb_ref, cya_ref, cyb_ref,
    out_ref, xa_ref, xb_ref, ya_ref, yb_ref, state_ref, halves_ref, edge_ref,
):
    state_ref[...] = field_ref[...]
    add_faces(state_ref, (cxa_ref, cxb_ref), (cya_ref, cyb_ref), sides("gx"), sides("gy"))
    step(state_ref, lists_ref, out_ref, halves_ref, edge_ref)
    take_faces(out_ref, (xa_ref, xb_ref), (ya_ref, yb_ref))


def last_y_kernel(
    part_ref, gya_ref, gyb_ref, mya_ref, myb_ref, oya_ref, oyb_ref, fya_ref, fyb_ref,
    out_ref, cya_ref, cyb_ref, rows_ref, sems,
):
    del part_ref
    odd = lax.axis_index("gy") & 1
    for n, (got, match, own, face, out) in enumerate((
        (gya_ref, mya_ref, oya_ref, fya_ref, cya_ref),
        (gyb_ref, myb_ref, oyb_ref, fyb_ref, cyb_ref),
    )):
        remap(got, match, out, own)
        rows_ref[(odd + 1 + n) % 2] = (out[...] + face[...]).reshape(SLOTS, TILE, 1, NZ)
    copies = [
        pltpu.make_async_copy(rows_ref.at[i], out_ref.at[:, :, pl.ds(y, 1), :], sems.at[i])
        for i, y in enumerate((0, TILE - 1))
    ]
    for copy in copies:
        copy.start()
    for copy in copies:
        copy.wait()


def last_x_kernel(
    part_ref, gxa_ref, gxb_ref, mxa_ref, mxb_ref, fxa_ref, fxb_ref, cya_ref, cyb_ref,
    out_ref, face_ref, planes_ref, sems,
):
    del part_ref
    odd = lax.axis_index("gx") & 1
    for n, (got, match, face, x) in enumerate(
        zip((gxa_ref, gxb_ref), (mxa_ref, mxb_ref), (fxa_ref, fxb_ref), sides("gx"))
    ):
        remap(got, match, face_ref)
        add_rows(face_ref, x, (cya_ref, cyb_ref), sides("gy"))
        planes_ref[(odd + 1 + n) % 2] = (face_ref[...] + face[...]).reshape(SLOTS, 1, TILE, NZ)
    copies = [
        pltpu.make_async_copy(planes_ref.at[i], out_ref.at[:, pl.ds(x, 1), :, :], sems.at[i])
        for i, x in enumerate((0, TILE - 1))
    ]
    for copy in copies:
        copy.start()
    for copy in copies:
        copy.wait()


def call(body, outs, scratch=(), flops=0, bytes_accessed=0, vmem=40, **specs):
    return pl.pallas_call(
        body,
        out_shape=[jax.ShapeDtypeStruct(shape, F32) for shape in outs],
        scratch_shapes=[pltpu.VMEM(*one) if isinstance(one, tuple) else one for one in scratch],
        compiler_params=pltpu.CompilerParams(vmem_limit_bytes=vmem * 2**20),
        cost_estimate=pl.CostEstimate(
            flops=flops, bytes_accessed=bytes_accessed, transcendentals=0
        ),
        **specs,
    )


def pairs(count, start):
    order = []
    for i in range(start, start + count, 2):
        a, b = i % count, (i + 1) % count
        order += [(a, b), (b, a)]
    return order


def exchange(value, axis, which):
    return lax.ppermute(value, axis, pairs(lax.axis_size(axis), which))


WHOLE = (SLOTS, ROWS, NZ)
SIDE = (FACE, NZ)
FIRST = (HEAD, NZ)
SECOND = (PART, NZ)
LISTS = (SLOTS + 8, NZ)
STEP_SCRATCH = [((SLOTS, ROWS, 2 * NZ), BF16), ((ROWS, 4 * NZ), BF16)]
MATCH = (SLOTS, SLOTS, NZ)
ANYWHERE = pl.BlockSpec(memory_space=pl.ANY)
HERE = pl.BlockSpec(memory_space=pltpu.VMEM)


def shards(phase_fields, grain_ids):
    field = phase_fields.reshape(WHOLE)
    ids = grain_ids.reshape(NTZ, SLOTS)
    sxa, sxb, sya, syb = call(
        pack_kernel,
        [FIRST] * 4,
        [
            ((2, SLOTS, 1, TILE, NZ), F32),
            ((2, SLOTS, TILE, 1, NZ), F32),
            ((NTZ, SLOTS), jnp.int32),
            (SIDE, F32),
            pltpu.SemaphoreType.DMA((5,)),
        ],
        bytes_accessed=3 << 20,
        vmem=62,
        in_specs=[ANYWHERE, ANYWHERE],
    )(phase_fields, ids)
    gxa, gxb = exchange(sxa, "gx", 0), exchange(sxb, "gx", 1)
    gya, gyb = exchange(sya, "gy", 0), exchange(syb, "gy", 1)
    part, pxa, pxb, pya, pyb, oya, oyb, lists = call(
        first_kernel,
        [WHOLE] + [SIDE] * 6 + [LISTS],
        STEP_SCRATCH,
        flops=4 << 30,
        bytes_accessed=4 << 20,
    )(field, ids)
    tya, tyb, cxa, cxb, mxa, mxb = call(
        x_kernel, [SECOND] * 2 + [SIDE] * 2 + [MATCH] * 2, [(SIDE, F32)], bytes_accessed=1 << 20
    )(lists, gxa, gxb, pya, pyb)
    gpya, gpyb = exchange(tya, "gy", 0), exchange(tyb, "gy", 1)
    txa, txb, cya, cyb, mya, myb = call(
        y_kernel, [SECOND] * 2 + [SIDE] * 2 + [MATCH] * 2, [(SIDE, F32)], bytes_accessed=1 << 20
    )(lists, gya, gyb, pxa, pxb, cxa, cxb)
    gpxa, gpxb = exchange(txa, "gx", 0), exchange(txb, "gx", 1)
    part, fxa, fxb, fya, fyb = call(
        second_kernel,
        [WHOLE] + [SIDE] * 4,
        [(WHOLE, F32)] + STEP_SCRATCH,
        flops=4 << 30,
        bytes_accessed=5 << 20,
    )(part, lists, cxa, cxb, cya, cyb)
    part, cya, cyb = call(
        last_y_kernel,
        [phase_fields.shape] + [SIDE] * 2,
        [((2, SLOTS, TILE, 1, NZ), F32), pltpu.SemaphoreType.DMA((2,))],
        bytes_accessed=1 << 20,
        in_specs=[ANYWHERE] + [HERE] * 8,
        out_specs=[ANYWHERE, HERE, HERE],
        input_output_aliases={0: 0},
    )(part.reshape(phase_fields.shape), gpya, gpyb, mya, myb, oya, oyb, fya, fyb)
    (out,) = call(
        last_x_kernel,
        [phase_fields.shape],
        [(SIDE, F32), ((2, SLOTS, 1, TILE, NZ), F32), pltpu.SemaphoreType.DMA((2,))],
        bytes_accessed=1 << 20,
        in_specs=[ANYWHERE] + [HERE] * 8,
        out_specs=[ANYWHERE],
        input_output_aliases={0: 0},
    )(part, gpxa, gpxb, mxa, mxb, fxa, fxb, cya, cyb)
    return out


def solution(mesh):
    in_specs = (P(None, "gx", "gy", None), P("gx", "gy", None, None))
    out_specs = P(None, "gx", "gy", None)
    return jax.shard_map(shards, mesh=mesh, in_specs=in_specs, out_specs=out_specs, check_vma=False)
```

```python
import jax
import jax.numpy as jnp
from jax import lax
from jax.experimental import pallas as pl
from jax.experimental.pallas import tpu as pltpu
from jax.sharding import PartitionSpec as P

SLOTS = 16
TILE = 16
ROWS = TILE * TILE
NZ = 128
NTZ = NZ // TILE
FACE = SLOTS * TILE
SENT = SLOTS - 1
PART = SENT * TILE
HEAD = PART + 8
RATE = 0.025
HIGHEST = lax.Precision.HIGHEST
F32 = jnp.float32
BF16 = jnp.bfloat16


def iota(shape, dim):
    return lax.broadcasted_iota(jnp.int32, shape, dim)


def sides(axis):
    odd = lax.axis_index(axis) & 1
    return (TILE - 1) * (1 - odd), (TILE - 1) * odd


def flat_ids(ids):
    lane = iota((SLOTS, NZ), 1)
    spread = ((lane & 15) == iota((SLOTS, NZ), 0)).astype(F32)
    wide = jnp.dot(ids.astype(F32), spread, precision=HIGHEST, preferred_element_type=F32)
    own = (iota((NTZ, NZ), 1) >> 4) == iota((NTZ, NZ), 0)
    return jnp.sum(jnp.where(own, wide, 0.0), axis=0, keepdims=True)


def lane_ids(flat):
    pick = jnp.where((iota((SLOTS, NZ), 1) & 15) == iota((SLOTS, NZ), 0), flat, 0.0)
    group = ((iota((NZ, NZ), 0) >> 4) == (iota((NZ, NZ), 1) >> 4)).astype(F32)
    return jnp.dot(pick, group, precision=HIGHEST, preferred_element_type=F32)


def kept(mine):
    rows = []
    for s in range(SENT):
        row = jnp.where(mine[s : s + 1, :] >= 0.0, 1.0, 0.0)
        rows.append(row * rows[-1] if rows else row)
    return rows


def sent_ids(ids):
    rows = [
        jnp.where(row > 0.0, ids[s : s + 1, :], ids[s + 1 : s + 2, :])
        for s, row in enumerate(kept(ids))
    ]
    return jnp.concatenate(rows + [jnp.full((1, NZ), -2.0, F32)], axis=0)


def send(face_ref, mine, out_ref):
    for s, row in enumerate(kept(mine)):
        keep = jnp.broadcast_to(row, (TILE, NZ)) > 0.0
        here, after = (face_ref[t * TILE : (t + 1) * TILE, :] for t in (s, s + 1))
        out_ref[s * TILE : (s + 1) * TILE, :] = jnp.where(keep, here, after)


def matches(mine, other, match_ref):
    for s in range(SLOTS):
        row = mine[s : s + 1, :]
        match_ref[s] = jnp.where((other == row) & (row >= 0.0), RATE, 0.0)


def remap(plane, match_ref, out_ref, own_ref=None, count=SENT):
    for s in range(SLOTS):
        total = None
        if own_ref is not None:
            listed = RATE * jnp.sum(match_ref[s], axis=0, keepdims=True)
            total = listed * own_ref[s * TILE : (s + 1) * TILE, :]
        for t in range(count):
            term = match_ref[s, t : t + 1, :] * plane[t * TILE : (t + 1) * TILE, :]
            total = term if total is None else total + term
        out_ref[s * TILE : (s + 1) * TILE, :] = total


def take_x(field_ref, x):
    return field_ref[:, pl.ds(pl.multiple_of(x * TILE, TILE), TILE), :].reshape(FACE, NZ)


def take_y(field_ref, s, y):
    return field_ref[s, pl.ds(y, TILE, stride=TILE), :]


def add_faces(field_ref, x_faces, y_faces, xs, ys):
    for ref, x in zip(x_faces, xs):
        at = pl.ds(pl.multiple_of(x * TILE, TILE), TILE)
        field_ref[:, at, :] += ref[...].reshape(SLOTS, TILE, NZ)
    for ref, y in zip(y_faces, ys):
        for s in range(SLOTS):
            at = pl.ds(y, TILE, stride=TILE)
            field_ref[s, at, :] += ref[s * TILE : (s + 1) * TILE, :]


def step(field_ref, lists_ref, out_ref, halves_ref, edge_ref):
    flat = lists_ref[SLOTS : SLOTS + 1, :]
    for s in range(SLOTS):
        value = field_ref[s]
        high = value.astype(BF16)
        halves_ref[s, :, :NZ] = high
        halves_ref[s, :, NZ:] = (value - high.astype(F32)).astype(BF16)
    r, c = iota((2 * NZ, 2 * NZ), 0), iota((2 * NZ, 2 * NZ), 1)
    rz, cz = r & (NZ - 1), c & (NZ - 1)
    at = rz == (cz >> 4) * TILE + jnp.where(c < NZ, TILE - 1, 0)
    edges = jnp.zeros((ROWS, 2 * NZ), F32)
    for t in range(SLOTS):
        pick = jnp.where(at & ((c & 15) == t), 1.0, 0.0).astype(BF16)
        edges += jnp.dot(halves_ref[t], pick, preferred_element_type=F32)
    high = edges.astype(BF16)
    edge_ref[:, : 2 * NZ] = high
    edge_ref[:, 2 * NZ :] = (edges - high.astype(F32)).astype(BF16)
    eye = iota((NZ, NZ), 0) == iota((NZ, NZ), 1)
    column = jnp.sum(jnp.where(eye, flat, 0.0), axis=1, keepdims=True)
    column = jnp.concatenate([column, column], axis=0)
    row = jnp.concatenate([flat, flat], axis=1)
    hop = ((r >> 7) == (c >> 7)) & ((cz >> 4) == (((rz >> 4) + jnp.where(r < NZ, 1, 7)) & 7))
    match = jnp.where(hop & (column == row) & (column >= 0.0), 1.0, 0.0).astype(BF16)
    moved = jnp.dot(edge_ref[:, : 2 * NZ], match, preferred_element_type=F32)
    moved += jnp.dot(edge_ref[:, 2 * NZ :], match, preferred_element_type=F32)
    below, above = moved[:, :NZ], moved[:, NZ:]
    gap = jnp.abs(r - c)
    beside = (gap == TILE) | ((gap == 1) & ((r >> 4) == (c >> 4)))
    beside = jnp.where(beside, 1.0, 0.0).astype(BF16)
    r, c = iota((2 * NZ, NZ), 0) & (NZ - 1), iota((2 * NZ, NZ), 1)
    along = jnp.where((jnp.abs(r - c) == 1) & ((r >> 4) == (c >> 4)), 1.0, 0.0).astype(BF16)
    total = field_ref[0] * field_ref[0]
    for s in range(1, SLOTS):
        total += field_ref[s] * field_ref[s]
    base = 0.9 - 0.15 * total
    lane = iota((ROWS, NZ), 1) & 15
    for s in range(SLOTS):
        low = turn(below, -s)
        near = jnp.where(lane == 0, low, jnp.where(lane == TILE - 1, turn(above, TILE - 1 - s), 0.0))
        near += jnp.dot(halves_ref[s], along, preferred_element_type=F32)
        plane = jnp.dot(beside, halves_ref[s], preferred_element_type=F32)
        near += plane[:, :NZ] + plane[:, NZ:]
        value = field_ref[s]
        out_ref[s] = value * (base + 0.1 * (value * value)) + RATE * near


def turn(value, by, dim=1):
    by %= value.shape[dim]
    return pltpu.roll(value, by, dim) if by else value


def pack_kernel(
    field_ref, ids_ref, xa_ref, xb_ref, ya_ref, yb_ref, planes_ref, rows_ref, ids_vmem, face_ref, sems
):
    ids = pltpu.make_async_copy(ids_ref, ids_vmem, sems.at[4])
    planes = [
        pltpu.make_async_copy(field_ref.at[:, pl.ds(x, 1), :, :], planes_ref.at[i], sems.at[i])
        for i, x in enumerate((0, TILE - 1))
    ]
    rows = [
        pltpu.make_async_copy(field_ref.at[:, :, pl.ds(y, 1), :], rows_ref.at[i], sems.at[2 + i])
        for i, y in enumerate((0, TILE - 1))
    ]
    for copy in [ids] + planes + rows:
        copy.start()
    ids.wait()
    flat = flat_ids(ids_vmem[...])
    mine = lane_ids(flat)
    flat = jnp.broadcast_to(flat, (HEAD - PART, NZ))
    for copies, from_ref, refs, axis in (
        (planes, planes_ref, (xa_ref, xb_ref), "gx"),
        (rows, rows_ref, (ya_ref, yb_ref), "gy"),
    ):
        odd = lax.axis_index(axis) & 1
        for copy in copies:
            copy.wait()
        for n, ref in enumerate(refs):
            face_ref[...] = from_ref[(odd + 1 + n) % 2].reshape(FACE, NZ)
            send(face_ref, mine, ref)
            ref[PART:, :] = flat


def take_faces(field_ref, x_refs, y_refs):
    for ref, side in zip(x_refs, sides("gx")):
        ref[...] = take_x(field_ref, side)
    for ref, side in zip(y_refs, sides("gy")):
        for s in range(SLOTS):
            ref[s * TILE : (s + 1) * TILE, :] = take_y(field_ref, s, side)


def first_kernel(
    field_ref, ids_ref, out_ref, xa_ref, xb_ref, ya_ref, yb_ref, oya_ref, oyb_ref, lists_ref, halves_ref, edge_ref
):
    flat = flat_ids(ids_ref[...])
    lists_ref[:SLOTS, :] = lane_ids(flat)
    lists_ref[SLOTS:, :] = jnp.broadcast_to(flat, (8, NZ))
    step(field_ref, lists_ref, out_ref, halves_ref, edge_ref)
    take_faces(field_ref, (), (oya_ref, oyb_ref))
    take_faces(out_ref, (xa_ref, xb_ref), (ya_ref, yb_ref))


def arrive(lists_ref, gots, matchs, outs):
    for got, match, out in zip(gots, matchs, outs):
        matches(lists_ref[:SLOTS, :], sent_ids(lane_ids(got[PART : PART + 1, :])), match)
        remap(got, match, out)


def add_rows(out_ref, place, add_refs, add_places):
    for ref, there in zip(add_refs, add_places):
        out_ref[pl.ds(there, SLOTS, stride=TILE), :] += ref[pl.ds(place, SLOTS, stride=TILE), :]


def x_kernel(lists_ref, ga_ref, gb_ref, ya_ref, yb_ref, ya_out, yb_out, ca_ref, cb_ref, ma_ref, mb_ref, face_ref):
    arrive(lists_ref, (ga_ref, gb_ref), (ma_ref, mb_ref), (ca_ref, cb_ref))
    for out, part, y in zip((ya_out, yb_out), (ya_ref, yb_ref), sides("gy")):
        face_ref[...] = part[...]
        add_rows(face_ref, y, (ca_ref, cb_ref), sides("gx"))
        send(face_ref, lists_ref[:SLOTS, :], out)


def y_kernel(
    lists_ref, ga_ref, gb_ref, xa_ref, xb_ref, cxa_ref, cxb_ref,
    xa_out, xb_out, ca_ref, cb_ref, ma_ref, mb_ref, face_ref,
):
    arrive(lists_ref, (ga_ref, gb_ref), (ma_ref, mb_ref), (ca_ref, cb_ref))
    for out, part, add, x in zip((xa_out, xb_out), (xa_ref, xb_ref), (cxa_ref, cxb_ref), sides("gx")):
        face_ref[...] = part[...] + add[...]
        add_rows(face_ref, x, (ca_ref, cb_ref), sides("gy"))
        send(face_ref, lists_ref[:SLOTS, :], out)


def second_kernel(
    field_ref, lists_ref, cxa_ref, cxb_ref, cya_ref, cyb_ref,
    out_ref, xa_ref, xb_ref, ya_ref, yb_ref, state_ref, halves_ref, edge_ref,
):
    state_ref[...] = field_ref[...]
    add_faces(state_ref, (cxa_ref, cxb_ref), (cya_ref, cyb_ref), sides("gx"), sides("gy"))
    step(state_ref, lists_ref, out_ref, halves_ref, edge_ref)
    take_faces(out_ref, (xa_ref, xb_ref), (ya_ref, yb_ref))


def last_y_kernel(
    gya_ref, gyb_ref, mya_ref, myb_ref, oya_ref, oyb_ref, fya_ref, fyb_ref, ya_ref, yb_ref, cya_ref, cyb_ref
):
    for got, match, own, face, ref, out in (
        (gya_ref, mya_ref, oya_ref, fya_ref, ya_ref, cya_ref),
        (gyb_ref, myb_ref, oyb_ref, fyb_ref, yb_ref, cyb_ref),
    ):
        remap(got, match, out, own)
        ref[...] = out[...] + face[...]


def last_kernel(
    part_ref, gxa_ref, gxb_ref, mxa_ref, mxb_ref, fxa_ref, fxb_ref, ya_ref, yb_ref, cya_ref, cyb_ref,
    out_ref, face_ref, planes_ref, rows_ref, sems,
):
    del part_ref
    odd = lax.axis_index("gy") & 1
    for n, ref in enumerate((ya_ref, yb_ref)):
        rows_ref[(odd + 1 + n) % 2] = ref[...].reshape(SLOTS, TILE, 1, NZ)
    rows = [
        pltpu.make_async_copy(rows_ref.at[i], out_ref.at[:, :, pl.ds(y, 1), :], sems.at[i])
        for i, y in enumerate((0, TILE - 1))
    ]
    for copy in rows:
        copy.start()
    odd = lax.axis_index("gx") & 1
    for n, (got, match, face, x) in enumerate(
        zip((gxa_ref, gxb_ref), (mxa_ref, mxb_ref), (fxa_ref, fxb_ref), sides("gx"))
    ):
        remap(got, match, face_ref)
        add_rows(face_ref, x, (cya_ref, cyb_ref), sides("gy"))
        planes_ref[(odd + 1 + n) % 2] = (face_ref[...] + face[...]).reshape(SLOTS, 1, TILE, NZ)
    for copy in rows:
        copy.wait()
    planes = [
        pltpu.make_async_copy(planes_ref.at[i], out_ref.at[:, pl.ds(x, 1), :, :], sems.at[2 + i])
        for i, x in enumerate((0, TILE - 1))
    ]
    for copy in planes:
        copy.start()
    for copy in planes:
        copy.wait()


def call(body, outs, scratch=(), flops=0, bytes_accessed=0, vmem=40, **specs):
    return pl.pallas_call(
        body,
        out_shape=[jax.ShapeDtypeStruct(shape, F32) for shape in outs],
        scratch_shapes=[pltpu.VMEM(*one) if isinstance(one, tuple) else one for one in scratch],
        compiler_params=pltpu.CompilerParams(vmem_limit_bytes=vmem * 2**20),
        cost_estimate=pl.CostEstimate(
            flops=flops, bytes_accessed=bytes_accessed, transcendentals=0
        ),
        **specs,
    )


def pairs(count, start):
    order = []
    for i in range(start, start + count, 2):
        a, b = i % count, (i + 1) % count
        order += [(a, b), (b, a)]
    return order


def exchange(value, axis, which):
    return lax.ppermute(value, axis, pairs(lax.axis_size(axis), which))


WHOLE = (SLOTS, ROWS, NZ)
SIDE = (FACE, NZ)
FIRST = (HEAD, NZ)
SECOND = (PART, NZ)
LISTS = (SLOTS + 8, NZ)
STEP_SCRATCH = [((SLOTS, ROWS, 2 * NZ), BF16), ((ROWS, 4 * NZ), BF16)]
MATCH = (SLOTS, SLOTS, NZ)
ANYWHERE = pl.BlockSpec(memory_space=pl.ANY)
HERE = pl.BlockSpec(memory_space=pltpu.VMEM)


def shards(phase_fields, grain_ids):
    field = phase_fields.reshape(WHOLE)
    ids = grain_ids.reshape(NTZ, SLOTS)
    sxa, sxb, sya, syb = call(
        pack_kernel,
        [FIRST] * 4,
        [
            ((2, SLOTS, 1, TILE, NZ), F32),
            ((2, SLOTS, TILE, 1, NZ), F32),
            ((NTZ, SLOTS), jnp.int32),
            (SIDE, F32),
            pltpu.SemaphoreType.DMA((5,)),
        ],
        bytes_accessed=3 << 20,
        vmem=62,
        in_specs=[ANYWHERE, ANYWHERE],
    )(phase_fields, ids)
    gxa, gxb = exchange(sxa, "gx", 0), exchange(sxb, "gx", 1)
    gya, gyb = exchange(sya, "gy", 0), exchange(syb, "gy", 1)
    part, pxa, pxb, pya, pyb, oya, oyb, lists = call(
        first_kernel,
        [WHOLE] + [SIDE] * 6 + [LISTS],
        STEP_SCRATCH,
        flops=4 << 30,
        bytes_accessed=4 << 20,
    )(field, ids)
    tya, tyb, cxa, cxb, mxa, mxb = call(
        x_kernel, [SECOND] * 2 + [SIDE] * 2 + [MATCH] * 2, [(SIDE, F32)], bytes_accessed=1 << 20
    )(lists, gxa, gxb, pya, pyb)
    gpya, gpyb = exchange(tya, "gy", 0), exchange(tyb, "gy", 1)
    txa, txb, cya, cyb, mya, myb = call(
        y_kernel, [SECOND] * 2 + [SIDE] * 2 + [MATCH] * 2, [(SIDE, F32)], bytes_accessed=1 << 20
    )(lists, gya, gyb, pxa, pxb, cxa, cxb)
    gpxa, gpxb = exchange(txa, "gx", 0), exchange(txb, "gx", 1)
    part, fxa, fxb, fya, fyb = call(
        second_kernel,
        [WHOLE] + [SIDE] * 4,
        [(WHOLE, F32)] + STEP_SCRATCH,
        flops=4 << 30,
        bytes_accessed=5 << 20,
    )(part, lists, cxa, cxb, cya, cyb)
    fya, fyb, cya, cyb = call(last_y_kernel, [SIDE] * 4, bytes_accessed=1 << 20)(
        gpya, gpyb, mya, myb, oya, oyb, fya, fyb
    )
    (out,) = call(
        last_kernel,
        [phase_fields.shape],
        [
            (SIDE, F32),
            ((2, SLOTS, 1, TILE, NZ), F32),
            ((2, SLOTS, TILE, 1, NZ), F32),
            pltpu.SemaphoreType.DMA((4,)),
        ],
        bytes_accessed=1 << 20,
        in_specs=[ANYWHERE] + [HERE] * 10,
        out_specs=[ANYWHERE],
        input_output_aliases={0: 0},
    )(part.reshape(phase_fields.shape), gpxa, gpxb, mxa, mxb, fxa, fxb, fya, fyb, cya, cyb)
    return out


def solution(mesh):
    in_specs = (P(None, "gx", "gy", None), P("gx", "gy", None, None))
    out_specs = P(None, "gx", "gy", None)
    return jax.shard_map(shards, mesh=mesh, in_specs=in_specs, out_specs=out_specs, check_vma=False)
```

```python
import jax
import jax.numpy as jnp
from jax import lax
from jax.experimental import pallas as pl
from jax.experimental.pallas import tpu as pltpu
from jax.sharding import PartitionSpec as P

SLOTS = 16
TILE = 16
ROWS = TILE * TILE
NZ = 128
NTZ = NZ // TILE
FACE = SLOTS * TILE
SENT = SLOTS - 1
PART = SENT * TILE
HEAD = PART + 8
RATE = 0.025
HIGHEST = lax.Precision.HIGHEST
F32 = jnp.float32
BF16 = jnp.bfloat16


def iota(shape, dim):
    return lax.broadcasted_iota(jnp.int32, shape, dim)


def sides(axis):
    odd = lax.axis_index(axis) & 1
    return (TILE - 1) * (1 - odd), (TILE - 1) * odd


def flat_ids(ids):
    lane = iota((SLOTS, NZ), 1)
    spread = ((lane & 15) == iota((SLOTS, NZ), 0)).astype(F32)
    wide = jnp.dot(ids.astype(F32), spread, precision=HIGHEST, preferred_element_type=F32)
    own = (iota((NTZ, NZ), 1) >> 4) == iota((NTZ, NZ), 0)
    return jnp.sum(jnp.where(own, wide, 0.0), axis=0, keepdims=True)


def lane_ids(flat):
    pick = jnp.where((iota((SLOTS, NZ), 1) & 15) == iota((SLOTS, NZ), 0), flat, 0.0)
    group = ((iota((NZ, NZ), 0) >> 4) == (iota((NZ, NZ), 1) >> 4)).astype(F32)
    return jnp.dot(pick, group, precision=HIGHEST, preferred_element_type=F32)


def kept(mine):
    rows = []
    for s in range(SENT):
        row = jnp.where(mine[s : s + 1, :] >= 0.0, 1.0, 0.0)
        rows.append(row * rows[-1] if rows else row)
    return rows


def sent_ids(ids):
    rows = [
        jnp.where(row > 0.0, ids[s : s + 1, :], ids[s + 1 : s + 2, :])
        for s, row in enumerate(kept(ids))
    ]
    return jnp.concatenate(rows + [jnp.full((1, NZ), -2.0, F32)], axis=0)


def send(face_ref, mine, out_ref):
    for s, row in enumerate(kept(mine)):
        keep = jnp.broadcast_to(row, (TILE, NZ)) > 0.0
        here, after = (face_ref[t * TILE : (t + 1) * TILE, :] for t in (s, s + 1))
        out_ref[s * TILE : (s + 1) * TILE, :] = jnp.where(keep, here, after)


def matches(mine, other, match_ref):
    for s in range(SLOTS):
        row = mine[s : s + 1, :]
        match_ref[s] = jnp.where((other == row) & (row >= 0.0), RATE, 0.0)


def remap(plane, match_ref, out_ref, own_ref=None, count=SENT):
    for s in range(SLOTS):
        total = None
        if own_ref is not None:
            listed = RATE * jnp.sum(match_ref[s], axis=0, keepdims=True)
            total = listed * own_ref[s * TILE : (s + 1) * TILE, :]
        for t in range(count):
            term = match_ref[s, t : t + 1, :] * plane[t * TILE : (t + 1) * TILE, :]
            total = term if total is None else total + term
        out_ref[s * TILE : (s + 1) * TILE, :] = total


def take_x(field_ref, x):
    return field_ref[:, pl.ds(pl.multiple_of(x * TILE, TILE), TILE), :].reshape(FACE, NZ)


def take_y(field_ref, s, y):
    return field_ref[s, pl.ds(y, TILE, stride=TILE), :]


def add_faces(field_ref, x_faces, y_faces, xs, ys):
    for ref, x in zip(x_faces, xs):
        at = pl.ds(pl.multiple_of(x * TILE, TILE), TILE)
        field_ref[:, at, :] += ref[...].reshape(SLOTS, TILE, NZ)
    for ref, y in zip(y_faces, ys):
        for s in range(SLOTS):
            at = pl.ds(y, TILE, stride=TILE)
            field_ref[s, at, :] += ref[s * TILE : (s + 1) * TILE, :]


def step(field_ref, lists_ref, out_ref, halves_ref, edge_ref):
    flat = lists_ref[SLOTS : SLOTS + 1, :]
    for s in range(SLOTS):
        value = field_ref[s]
        high = value.astype(BF16)
        halves_ref[s, :, :NZ] = high
        halves_ref[s, :, NZ:] = (value - high.astype(F32)).astype(BF16)
    r, c = iota((2 * NZ, 2 * NZ), 0), iota((2 * NZ, 2 * NZ), 1)
    rz, cz = r & (NZ - 1), c & (NZ - 1)
    at = rz == (cz >> 4) * TILE + jnp.where(c < NZ, TILE - 1, 0)
    edges = jnp.zeros((ROWS, 2 * NZ), F32)
    for t in range(SLOTS):
        pick = jnp.where(at & ((c & 15) == t), 1.0, 0.0).astype(BF16)
        edges += jnp.dot(halves_ref[t], pick, preferred_element_type=F32)
    high = edges.astype(BF16)
    edge_ref[:, : 2 * NZ] = high
    edge_ref[:, 2 * NZ :] = (edges - high.astype(F32)).astype(BF16)
    eye = iota((NZ, NZ), 0) == iota((NZ, NZ), 1)
    column = jnp.sum(jnp.where(eye, flat, 0.0), axis=1, keepdims=True)
    column = jnp.concatenate([column, column], axis=0)
    row = jnp.concatenate([flat, flat], axis=1)
    hop = ((r >> 7) == (c >> 7)) & ((cz >> 4) == (((rz >> 4) + jnp.where(r < NZ, 1, 7)) & 7))
    match = jnp.where(hop & (column == row) & (column >= 0.0), 1.0, 0.0).astype(BF16)
    moved = jnp.dot(edge_ref[:, : 2 * NZ], match, preferred_element_type=F32)
    moved += jnp.dot(edge_ref[:, 2 * NZ :], match, preferred_element_type=F32)
    below, above = moved[:, :NZ], moved[:, NZ:]
    gap = jnp.abs(r - c)
    beside = (gap == TILE) | ((gap == 1) & ((r >> 4) == (c >> 4)))
    beside = jnp.where(beside, 1.0, 0.0).astype(BF16)
    r, c = iota((2 * NZ, NZ), 0) & (NZ - 1), iota((2 * NZ, NZ), 1)
    along = jnp.where((jnp.abs(r - c) == 1) & ((r >> 4) == (c >> 4)), 1.0, 0.0).astype(BF16)
    total = field_ref[0] * field_ref[0]
    for s in range(1, SLOTS):
        total += field_ref[s] * field_ref[s]
    base = 0.9 - 0.15 * total
    lane = iota((ROWS, NZ), 1) & 15
    for s in range(SLOTS):
        low = turn(below, -s)
        near = jnp.where(lane == 0, low, jnp.where(lane == TILE - 1, turn(above, TILE - 1 - s), 0.0))
        near += jnp.dot(halves_ref[s], along, preferred_element_type=F32)
        plane = jnp.dot(beside, halves_ref[s], preferred_element_type=F32)
        near += plane[:, :NZ] + plane[:, NZ:]
        value = field_ref[s]
        out_ref[s] = value * (base + 0.1 * (value * value)) + RATE * near


def turn(value, by, dim=1):
    by %= value.shape[dim]
    return pltpu.roll(value, by, dim) if by else value


def pack_kernel(
    field_ref, ids_ref, xa_ref, xb_ref, ya_ref, yb_ref, planes_ref, rows_ref, ids_vmem, face_ref, sems
):
    ids = pltpu.make_async_copy(ids_ref, ids_vmem, sems.at[4])
    planes = [
        pltpu.make_async_copy(field_ref.at[:, pl.ds(x, 1), :, :], planes_ref.at[i], sems.at[i])
        for i, x in enumerate((0, TILE - 1))
    ]
    rows = [
        pltpu.make_async_copy(field_ref.at[:, :, pl.ds(y, 1), :], rows_ref.at[i], sems.at[2 + i])
        for i, y in enumerate((0, TILE - 1))
    ]
    for copy in [ids] + planes + rows:
        copy.start()
    ids.wait()
    flat = flat_ids(ids_vmem[...])
    mine = lane_ids(flat)
    flat = jnp.broadcast_to(flat, (HEAD - PART, NZ))
    for copies, from_ref, refs, axis in (
        (planes, planes_ref, (xa_ref, xb_ref), "gx"),
        (rows, rows_ref, (ya_ref, yb_ref), "gy"),
    ):
        odd = lax.axis_index(axis) & 1
        for copy in copies:
            copy.wait()
        for n, ref in enumerate(refs):
            face_ref[...] = from_ref[(odd + 1 + n) % 2].reshape(FACE, NZ)
            send(face_ref, mine, ref)
            ref[PART:, :] = flat


def take_faces(field_ref, x_refs, y_refs):
    for ref, side in zip(x_refs, sides("gx")):
        ref[...] = take_x(field_ref, side)
    for ref, side in zip(y_refs, sides("gy")):
        for s in range(SLOTS):
            ref[s * TILE : (s + 1) * TILE, :] = take_y(field_ref, s, side)


def first_kernel(
    field_ref, ids_ref, out_ref, xa_ref, xb_ref, ya_ref, yb_ref, lists_ref, halves_ref, edge_ref
):
    flat = flat_ids(ids_ref[...])
    lists_ref[:SLOTS, :] = lane_ids(flat)
    lists_ref[SLOTS:, :] = jnp.broadcast_to(flat, (8, NZ))
    step(field_ref, lists_ref, out_ref, halves_ref, edge_ref)
    take_faces(out_ref, (xa_ref, xb_ref), (ya_ref, yb_ref))


def arrive(lists_ref, gots, matchs, outs):
    for got, match, out in zip(gots, matchs, outs):
        matches(lists_ref[:SLOTS, :], sent_ids(lane_ids(got[PART : PART + 1, :])), match)
        remap(got, match, out)


def add_rows(out_ref, place, add_refs, add_places):
    for ref, there in zip(add_refs, add_places):
        out_ref[pl.ds(there, SLOTS, stride=TILE), :] += ref[pl.ds(place, SLOTS, stride=TILE), :]


def x_kernel(lists_ref, ga_ref, gb_ref, ya_ref, yb_ref, ya_out, yb_out, ca_ref, cb_ref, ma_ref, mb_ref, face_ref):
    arrive(lists_ref, (ga_ref, gb_ref), (ma_ref, mb_ref), (ca_ref, cb_ref))
    for out, part, y in zip((ya_out, yb_out), (ya_ref, yb_ref), sides("gy")):
        face_ref[...] = part[...]
        add_rows(face_ref, y, (ca_ref, cb_ref), sides("gx"))
        send(face_ref, lists_ref[:SLOTS, :], out)


def y_kernel(
    lists_ref, ga_ref, gb_ref, xa_ref, xb_ref, cxa_ref, cxb_ref,
    xa_out, xb_out, ca_ref, cb_ref, ma_ref, mb_ref, face_ref,
):
    arrive(lists_ref, (ga_ref, gb_ref), (ma_ref, mb_ref), (ca_ref, cb_ref))
    for out, part, add, x in zip((xa_out, xb_out), (xa_ref, xb_ref), (cxa_ref, cxb_ref), sides("gx")):
        face_ref[...] = part[...] + add[...]
        add_rows(face_ref, x, (ca_ref, cb_ref), sides("gy"))
        send(face_ref, lists_ref[:SLOTS, :], out)


def second_kernel(
    field_ref, start_ref, lists_ref, cxa_ref, cxb_ref, cya_ref, cyb_ref,
    out_ref, xa_ref, xb_ref, ya_ref, yb_ref, oya_ref, oyb_ref, state_ref, halves_ref, edge_ref,
):
    take_faces(start_ref, (), (oya_ref, oyb_ref))
    state_ref[...] = field_ref[...]
    add_faces(state_ref, (cxa_ref, cxb_ref), (cya_ref, cyb_ref), sides("gx"), sides("gy"))
    step(state_ref, lists_ref, out_ref, halves_ref, edge_ref)
    take_faces(out_ref, (xa_ref, xb_ref), (ya_ref, yb_ref))


def last_y_kernel(
    gya_ref, gyb_ref, mya_ref, myb_ref, oya_ref, oyb_ref, fya_ref, fyb_ref, ya_ref, yb_ref, cya_ref, cyb_ref
):
    for got, match, own, face, ref, out in (
        (gya_ref, mya_ref, oya_ref, fya_ref, ya_ref, cya_ref),
        (gyb_ref, myb_ref, oyb_ref, fyb_ref, yb_ref, cyb_ref),
    ):
        remap(got, match, out, own)
        ref[...] = out[...] + face[...]


def last_kernel(
    part_ref, gxa_ref, gxb_ref, mxa_ref, mxb_ref, fxa_ref, fxb_ref, ya_ref, yb_ref, cya_ref, cyb_ref,
    out_ref, face_ref, planes_ref, rows_ref, sems,
):
    del part_ref
    odd = lax.axis_index("gy") & 1
    for n, ref in enumerate((ya_ref, yb_ref)):
        rows_ref[(odd + 1 + n) % 2] = ref[...].reshape(SLOTS, TILE, 1, NZ)
    rows = [
        pltpu.make_async_copy(rows_ref.at[i], out_ref.at[:, :, pl.ds(y, 1), :], sems.at[i])
        for i, y in enumerate((0, TILE - 1))
    ]
    for copy in rows:
        copy.start()
    odd = lax.axis_index("gx") & 1
    for n, (got, match, face, x) in enumerate(
        zip((gxa_ref, gxb_ref), (mxa_ref, mxb_ref), (fxa_ref, fxb_ref), sides("gx"))
    ):
        remap(got, match, face_ref)
        add_rows(face_ref, x, (cya_ref, cyb_ref), sides("gy"))
        planes_ref[(odd + 1 + n) % 2] = (face_ref[...] + face[...]).reshape(SLOTS, 1, TILE, NZ)
    for copy in rows:
        copy.wait()
    planes = [
        pltpu.make_async_copy(planes_ref.at[i], out_ref.at[:, pl.ds(x, 1), :, :], sems.at[2 + i])
        for i, x in enumerate((0, TILE - 1))
    ]
    for copy in planes:
        copy.start()
    for copy in planes:
        copy.wait()


def call(body, outs, scratch=(), flops=0, bytes_accessed=0, vmem=40, **specs):
    return pl.pallas_call(
        body,
        out_shape=[jax.ShapeDtypeStruct(shape, F32) for shape in outs],
        scratch_shapes=[pltpu.VMEM(*one) if isinstance(one, tuple) else one for one in scratch],
        compiler_params=pltpu.CompilerParams(vmem_limit_bytes=vmem * 2**20),
        cost_estimate=pl.CostEstimate(
            flops=flops, bytes_accessed=bytes_accessed, transcendentals=0
        ),
        **specs,
    )


def pairs(count, start):
    order = []
    for i in range(start, start + count, 2):
        a, b = i % count, (i + 1) % count
        order += [(a, b), (b, a)]
    return order


def exchange(value, axis, which):
    return lax.ppermute(value, axis, pairs(lax.axis_size(axis), which))


WHOLE = (SLOTS, ROWS, NZ)
SIDE = (FACE, NZ)
FIRST = (HEAD, NZ)
SECOND = (PART, NZ)
LISTS = (SLOTS + 8, NZ)
STEP_SCRATCH = [((SLOTS, ROWS, 2 * NZ), BF16), ((ROWS, 4 * NZ), BF16)]
MATCH = (SLOTS, SLOTS, NZ)
ANYWHERE = pl.BlockSpec(memory_space=pl.ANY)
HERE = pl.BlockSpec(memory_space=pltpu.VMEM)


def shards(phase_fields, grain_ids):
    field = phase_fields.reshape(WHOLE)
    ids = grain_ids.reshape(NTZ, SLOTS)
    sxa, sxb, sya, syb = call(
        pack_kernel,
        [FIRST] * 4,
        [
            ((2, SLOTS, 1, TILE, NZ), F32),
            ((2, SLOTS, TILE, 1, NZ), F32),
            ((NTZ, SLOTS), jnp.int32),
            (SIDE, F32),
            pltpu.SemaphoreType.DMA((5,)),
        ],
        bytes_accessed=3 << 20,
        vmem=62,
        in_specs=[ANYWHERE, ANYWHERE],
    )(phase_fields, ids)
    gxa, gxb = exchange(sxa, "gx", 0), exchange(sxb, "gx", 1)
    gya, gyb = exchange(sya, "gy", 0), exchange(syb, "gy", 1)
    part, pxa, pxb, pya, pyb, lists = call(
        first_kernel,
        [WHOLE] + [SIDE] * 4 + [LISTS],
        STEP_SCRATCH,
        flops=4 << 30,
        bytes_accessed=4 << 20,
    )(field, ids)
    tya, tyb, cxa, cxb, mxa, mxb = call(
        x_kernel, [SECOND] * 2 + [SIDE] * 2 + [MATCH] * 2, [(SIDE, F32)], bytes_accessed=1 << 20
    )(lists, gxa, gxb, pya, pyb)
    gpya, gpyb = exchange(tya, "gy", 0), exchange(tyb, "gy", 1)
    txa, txb, cya, cyb, mya, myb = call(
        y_kernel, [SECOND] * 2 + [SIDE] * 2 + [MATCH] * 2, [(SIDE, F32)], bytes_accessed=1 << 20
    )(lists, gya, gyb, pxa, pxb, cxa, cxb)
    gpxa, gpxb = exchange(txa, "gx", 0), exchange(txb, "gx", 1)
    part, fxa, fxb, fya, fyb, oya, oyb = call(
        second_kernel,
        [WHOLE] + [SIDE] * 6,
        [(WHOLE, F32)] + STEP_SCRATCH,
        flops=4 << 30,
        bytes_accessed=5 << 20,
    )(part, field, lists, cxa, cxb, cya, cyb)
    fya, fyb, cya, cyb = call(last_y_kernel, [SIDE] * 4, bytes_accessed=1 << 20)(
        gpya, gpyb, mya, myb, oya, oyb, fya, fyb
    )
    (out,) = call(
        last_kernel,
        [phase_fields.shape],
        [
            (SIDE, F32),
            ((2, SLOTS, 1, TILE, NZ), F32),
            ((2, SLOTS, TILE, 1, NZ), F32),
            pltpu.SemaphoreType.DMA((4,)),
        ],
        bytes_accessed=1 << 20,
        in_specs=[ANYWHERE] + [HERE] * 10,
        out_specs=[ANYWHERE],
        input_output_aliases={0: 0},
    )(part.reshape(phase_fields.shape), gpxa, gpxb, mxa, mxb, fxa, fxb, fya, fyb, cya, cyb)
    return out


def solution(mesh):
    in_specs = (P(None, "gx", "gy", None), P("gx", "gy", None, None))
    out_specs = P(None, "gx", "gy", None)
    return jax.shard_map(shards, mesh=mesh, in_specs=in_specs, out_specs=out_specs, check_vma=False)
```
